512 devices in a mesh: grp: 2 (over y_hi), seq: 32 (over z, core), dp: 8 (over x, y_lo).
Axes of the slice: x: 4, y: 4 (y_hi: 2, y_lo: 2; y = y_hi * 2 + y_lo), z: 16, core: 2. Of those that a mesh axis runs over, the one named last changes fastest.
Arguments:
- queries: bfloat16 [32, 2048, 2048], P(('grp', 'dp'), 'seq'), may hold values from -26 to 26
- key_states: bfloat16 [32, 2048, 2048], P(('grp', 'dp'), 'seq'), may hold values from -26 to 26
- value_states: bfloat16 [32, 2048, 2048], P(('grp', 'dp'), 'seq'), may hold values from -6 to 6
- projector: bfloat16 [2048, 1536], P('seq'), may hold values from -0.125 to 0.125
- teacher: bfloat16 [32, 2048, 1536], P(('grp', 'dp'), 'seq'), may hold values from -6 to 6
- enc_gain: float32 [1536], replicated, may hold values from 0.1 to 1.9
- enc_bias: float32 [1536], replicated, may hold values from -3 to 3
- valid_len: int32 [32], replicated, may hold values from 1 to 2048, 49152 in all
Outputs:
- grad_queries: bfloat16 [32, 2048, 2048], P(('grp', 'dp'), 'seq')
- grad_keys: bfloat16 [32, 2048, 2048], P(('grp', 'dp'), 'seq')
- grad_values: bfloat16 [32, 2048, 2048], P(('grp', 'dp'), 'seq')
The draws below stay inside these ranges and needn't reach their ends.
Inputs may be any that keep to these rules, and one draw needn't show every extreme that they name: valid_len[b] counts the leading real tokens of image b; some image has all 2048.
All inputs are finite; a program needn't handle non-finite values.
Results may differ from the reference program's by a relative error of at most 0.025.
Values may be sent and summed in bfloat16 or wider, within the bound.
A program may use at most 128 MiB of HBM per device.

```python
import math
import jax
import jax.numpy as jnp
import numpy as np
from jax import lax

HEADS = 16
HD = 128
ENC = 1536
S = 2048
DW = 2048
IMGS = 32


def draw_queries(key, part):
    key = jax.random.fold_in(key, 11)
    base = jax.random.normal(key, (IMGS, S, HEADS * HD), jnp.float32)
    return base.astype(jnp.bfloat16)


def draw_key_states(key, part):
    key = jax.random.fold_in(key, 23)
    base = jax.random.normal(key, (IMGS, S, HEADS * HD), jnp.float32)
    return base.astype(jnp.bfloat16)


def steps_of(key, shape, split, low, top_value):
    def one(axis_at, shards_of):
        draws = jax.random.uniform(jax.random.fold_in(jax.random.fold_in(key, 6), axis_at), (shards_of,), jnp.float32, low / len(split), top_value / len(split))
        return jnp.repeat(jnp.exp(draws), shape[axis_at] // shards_of).reshape((-1,) + (1,) * (len(shape) - axis_at - 1))

    loudness = one(*split[0])
    for cut in split[1:]:
        loudness = loudness * one(*cut)
    return loudness


def profile(amount, total, reach, skew):
    portions = [(1 << 20) // math.isqrt(standing ** skew) + 1 for standing in range(2, amount + 1)]
    spare, counts = total - reach - (amount - 1), [1] * (amount - 1)
    while spare > 0:
        free = [i for i in range(amount - 1) if counts[i] < reach]
        mass, left = sum([portions[i] for i in free]), spare
        for i in free:
            more = min(reach - counts[i], max(1, left * portions[i] // mass), spare)
            counts[i] = counts[i] + more
            spare = spare - more
    return np.array([reach] + counts)


def ragged_sizes(key, count, total, limit, lean):
    if count == 2:
        one = jax.random.randint(key, (), max(1, total - limit), min(limit, total - 1) + 1)
        return jnp.stack([one, total - one])
    lengths = jnp.asarray(profile(count, total, limit, lean), jnp.int32)
    pairs = (count - 1) // 2
    source_of, taker = lengths[1:1 + 2 * pairs:2], lengths[2:2 + 2 * pairs:2]
    slack = jnp.minimum(source_of - 1, limit - taker)
    passed = jax.random.randint(jax.random.fold_in(key, 1), (pairs,), 0, 1 << 20) % (slack + 1)
    lengths = lengths.at[1:1 + 2 * pairs:2].set(source_of - passed).at[2:2 + 2 * pairs:2].set(taker + passed)
    return lengths[jax.random.permutation(jax.random.fold_in(key, 2), count)]


def bell_draw(own_key, extent, deviation, reach, cuts=(), held_as=jnp.bfloat16):
    drawn = deviation * jax.random.normal(own_key, extent, jnp.float32)
    if cuts:
        drawn = drawn * steps_of(own_key, extent, cuts, -0.22, 0.18)
    return jnp.clip(drawn, -reach, reach).astype(held_as)


def setup_inputs(seed: int = 0) -> dict:
    seeds = jax.random.split(jax.random.key(seed), 9)
    queries = draw_queries(jax.random.fold_in(seeds[8], 71), 0)
    key_states = draw_key_states(jax.random.fold_in(seeds[8], 71), 0)
    value_states = bell_draw(seeds[2], (IMGS, S, DW), 1.0, 6.0, ((0, 16), (1, 32)))
    projector = bell_draw(seeds[3], (DW, ENC), DW ** -0.5, 0.125, ((0, 32),))
    teacher = bell_draw(seeds[4], (IMGS, S, ENC), 1.0, 6.0, ((0, 16), (1, 32)))
    enc_gain = jnp.clip(1.0 + 0.18 * jax.random.normal(seeds[5], (ENC,), jnp.float32), 0.1, 1.9)
    enc_bias = bell_draw(seeds[6], (ENC,), 0.5, 3.0, (), jnp.float32)
    valid_len = ragged_sizes(seeds[7], IMGS, IMGS * S * 3 // 4, S, 1).astype(jnp.int32)
    return {"queries": queries, "key_states": key_states, "value_states": value_states, "projector": projector, "teacher": teacher, "enc_gain": enc_gain, "enc_bias": enc_bias, "valid_len": valid_len}


EPS = 1e-06
COEF = 2048.0

def layer_norm(rows, gain, bias):
    data = rows.astype(jnp.float32)
    center = data - lax.optimization_barrier(jnp.mean(data, axis=-1, keepdims=True))
    spread = lax.optimization_barrier(jnp.mean(center * center, axis=-1, keepdims=True))
    return center * lax.rsqrt(spread + EPS) * gain.astype(jnp.float32) + bias.astype(jnp.float32)

def cosine_grad(aligned, target, keep):
    tgt = target.astype(jnp.float32)
    width = aligned.shape[-1]
    inner = lax.optimization_barrier(jnp.mean(aligned * tgt, axis=-1, keepdims=True))
    own = lax.optimization_barrier(jnp.mean(aligned * aligned, axis=-1, keepdims=True)) + EPS
    other = lax.optimization_barrier(jnp.mean(tgt * tgt, axis=-1, keepdims=True)) + EPS
    inverse = lax.rsqrt(own * other)
    cosine = inner * inverse
    return -COEF / width * keep[..., None] * (tgt * inverse - cosine / own * aligned)

def reference(queries, key_states, value_states, projector, teacher, enc_gain, enc_bias, valid_len):
    target = layer_norm(jnp.roll(teacher, IMGS // 2, axis=0), enc_gain, enc_bias).astype(jnp.bfloat16)
    scale = HD ** (-0.5)
    positions = jnp.arange(S, dtype=jnp.int32)

    def split_heads(rows):
        return rows.reshape(S, HEADS, HD).transpose(1, 0, 2).astype(jnp.float32)

    def join_heads(block):
        return block.transpose(1, 0, 2).reshape(S, HEADS * HD)

    def per_image(items):
        query, keyrow, value, tgt, length = items
        keep = positions < length
        qh = split_heads(query)
        kh = split_heads(keyrow)
        vh = split_heads(value)
        scores = jnp.einsum('hid,hjd->hij', qh, kh) * scale
        scores = jnp.where(keep[None, None, :], scores, -jnp.inf)
        top = lax.optimization_barrier(jnp.max(scores, axis=-1, keepdims=True))
        expo = jnp.exp(scores - top)
        probs = expo / lax.optimization_barrier(jnp.sum(expo, axis=-1, keepdims=True))
        probs_b = probs.astype(jnp.bfloat16).astype(jnp.float32)
        attended = jnp.einsum('hij,hjd->hid', probs_b, vh).astype(jnp.bfloat16)
        aligned = jnp.dot(join_heads(attended), projector, preferred_element_type=jnp.float32)
        grad_aligned = cosine_grad(aligned, tgt, keep.astype(jnp.float32)).astype(jnp.bfloat16)
        grad_att = jnp.dot(grad_aligned, projector.T, preferred_element_type=jnp.float32).astype(jnp.bfloat16)
        gh = split_heads(grad_att)
        grad_v = jnp.einsum('hij,hid->hjd', probs_b, gh).astype(jnp.bfloat16)
        grad_probs = jnp.einsum('hid,hjd->hij', gh, vh)
        delta = lax.optimization_barrier(jnp.sum(probs * grad_probs, axis=-1, keepdims=True))
        grad_scores = (probs * (grad_probs - delta) * scale).astype(jnp.bfloat16).astype(jnp.float32)
        grad_q = jnp.einsum('hij,hjd->hid', grad_scores, kh).astype(jnp.bfloat16)
        grad_k = jnp.einsum('hij,hid->hjd', grad_scores, qh).astype(jnp.bfloat16)
        return (join_heads(grad_q), join_heads(grad_k), join_heads(grad_v))
    grad_queries, grad_keys, grad_values = lax.map(per_image, (queries, key_states, value_states, target, valid_len))
    return (grad_queries, grad_keys, grad_values)
```

```python
import functools

import jax
import jax.numpy as jnp
from jax import lax
from jax.experimental import pallas as pl
from jax.experimental.pallas import tpu as pltpu
from jax.sharding import PartitionSpec as P

HD = 128
SEG = 64
TOK = 2 * SEG
EPS = 1e-06
COEF = 2048.0
LOG2E = 1.4426950408889634
MESH = pl.DeviceIdType.MESH
BF = jnp.bfloat16
F32 = jnp.float32
NT = (((1,), (1,)), ((), ()))


def al(value, step):
    return pl.multiple_of(value, step)


def kernel(
    nz, nr, ndp, bq,
    q_ref, k_ref, v_ref, w_ref, t_ref, gain_ref, bias_ref, kb_ref, keep_ref,
    oq_ref, ok_ref, ov_ref,
    qh, kh, va, wf, tea, att_h, rows, gsend, gh, gq_h, gk_h, gv_h,
    expo, att_f, linv, aligned, gal, acc_k, acc_v,
    in_send, in_recv, w_send, w_recv, t_send, t_recv, mid_send, mid_recv, out_send, out_recv,
):
    ns = 2 * nz
    total = ns * SEG
    enc = t_ref.shape[-1]
    cq = nr // 4
    cw = enc // cq
    nb = total // bq
    per = bq // TOK
    scale = HD ** (-0.5)

    me = lax.axis_index("seq")
    grp = lax.axis_index("grp")
    ring = grp * ndp + lax.axis_index("dp")
    z = me // 2
    c = lax.rem(me, 2)

    def on_ring(s):
        return {"seq": s}

    def in_plane(r):
        return {"grp": r // ndp, "dp": lax.rem(r, ndp)}

    def across(s):
        return {"grp": 1 - grp, "seq": s}

    barrier = pltpu.get_barrier_semaphore()

    def greet(device):
        pl.semaphore_signal(barrier, 1, device_id=device, device_id_type=MESH)

    @pl.loop(1, ns)
    def _(step):
        greet(on_ring(lax.rem(me + step, ns)))

    @pl.loop(1, nr)
    def _(step):
        greet(in_plane(lax.rem(ring + step, nr)))

    greet(across(2 * z + 1 - c))
    pl.semaphore_wait(barrier, ns - 1 + nr - 1 + 1)

    def remote(src, dst, ssem, rsem, device):
        return pltpu.make_async_remote_copy(
            src_ref=src, dst_ref=dst, send_sem=ssem, recv_sem=rsem, device_id=device, device_id_type=MESH
        )

    def waiting(view, sem):
        pltpu.make_async_copy(view, view, sem).wait()

    for image in range(2):
        remote(
            t_ref.at[image], tea.at[c], t_send, t_recv, across(2 * z + image)
        ).start()

    band = ring // cq
    wcols = pl.ds(al(lax.rem(ring, cq) * cw, 128), cw)
    own_w = w_ref.at[band, :, wcols]

    @pl.loop(1, nz)
    def _(step):
        there = lax.rem(z + step, nz)
        remote(
            own_w, wf.at[z, c, band, :, wcols], w_send.at[0], w_recv.at[0], on_ring(2 * there + c)
        ).start()

    pltpu.make_async_copy(own_w, wf.at[z, c, band, :, wcols], w_recv.at[0]).start()

    mine = pl.ds(al(me * SEG, SEG), SEG)
    sources = (k_ref, q_ref, v_ref)
    places = (kh.at[mine], qh.at[mine], va.at[mine, pl.ds(0, HD)])

    def send_inputs(image):
        for a in range(3):
            @pl.loop(1, nz)
            def _(step):
                there = lax.rem(z + step, nz)
                cols = pl.ds(al(there * HD, HD), HD)
                remote(
                    sources[a].at[image, :, cols], places[a], in_send.at[a], in_recv.at[a],
                    on_ring(2 * there + image),
                ).start()

            own = sources[a].at[image, :, pl.ds(al(z * HD, HD), HD)]

            @pl.when(c == image)
            def _():
                pltpu.make_async_copy(own, places[a], in_recv.at[a]).start()

            @pl.when(c != image)
            def _():
                remote(
                    own, places[a], in_send.at[a], in_recv.at[a], on_ring(2 * z + image)
                ).start()

    send_inputs(0)

    part_w = wf.at[:, c, band, :, wcols]
    waiting(part_w, w_recv.at[0])

    @pl.loop(1, nr)
    def _(step):
        remote(
            part_w, part_w, w_send.at[1], w_recv.at[1], in_plane(lax.rem(ring + step, nr))
        ).start()

    send_inputs(1)

    va[:, HD:] = jnp.ones((total, HD), BF)
    acc_k[...] = jnp.zeros_like(acc_k)
    acc_v[...] = jnp.zeros_like(acc_v)

    def swap_w():
        waiting(wf.at[pl.ds(0, nr - 1), c], w_recv.at[1])
        half = wf.at[:, c]
        remote(half, half, w_send.at[2], w_recv.at[2], on_ring(2 * z + 1 - c)).start()

    @pl.when(c == 1)
    def _():
        swap_w()

    waiting(tea, t_recv)
    for seg in range(2):
        data = tea[seg].astype(F32)
        center = data - jnp.mean(data, axis=-1, keepdims=True)
        spread = jnp.mean(center * center, axis=-1, keepdims=True)
        tea[seg] = (center * lax.rsqrt(spread + EPS) * gain_ref[...] + bias_ref[...]).astype(BF)

    waiting(kh, in_recv.at[0])
    waiting(qh, in_recv.at[1])
    waiting(va.at[:, pl.ds(0, HD)], in_recv.at[2])

    first = z // per

    @pl.loop(0, nb)
    def _(step):
        block = lax.rem(first + step, nb)
        span = pl.ds(al(block * bq, bq), bq)
        scores = lax.dot_general(qh[span], kh[...], NT, preferred_element_type=F32)
        scores = scores * (scale * LOG2E) + kb_ref[...]
        top = jnp.max(scores, axis=-1, keepdims=True)
        raised = jnp.exp2(scores - top).astype(BF)
        expo[span] = raised
        both = jnp.dot(raised, va[...], preferred_element_type=F32)
        inverse = 1.0 / both[:, HD:]
        attended = both[:, :HD] * inverse
        linv[span] = inverse
        att_f[span] = attended
        att_h[span] = attended.astype(BF)
        for part in range(per):
            there = block * per + part
            src = att_h.at[pl.ds(al(there * TOK, TOK), TOK)]
            dst = rows.at[:, pl.ds(al(z * HD, HD), HD)]

            @pl.when(there == z)
            def _():
                pltpu.make_async_copy(src, dst, mid_recv.at[0]).start()

            @pl.when(there != z)
            def _():
                remote(src, dst, mid_send.at[0], mid_recv.at[0], on_ring(2 * there + c)).start()

    @pl.when(c == 0)
    def _():
        swap_w()

    waiting(wf.at[:, 1 - c], w_recv.at[2])
    waiting(rows, mid_recv.at[0])

    pieces = enc // 384
    inner = jnp.zeros((TOK, 1), F32)
    own = jnp.zeros((TOK, 1), F32)
    other = jnp.zeros((TOK, 1), F32)
    for piece in range(pieces):
        cols = slice(piece * 384, (piece + 1) * 384)
        weights = wf[:, :, :, :, cols].reshape(nz * HD, 384)
        out = jnp.dot(rows[...], weights, preferred_element_type=F32)
        aligned[:, cols] = out
        tgt = tea[:, :, cols].reshape(TOK, 384).astype(F32)
        inner += jnp.sum(out * tgt, axis=-1, keepdims=True)
        own += jnp.sum(out * out, axis=-1, keepdims=True)
        other += jnp.sum(tgt * tgt, axis=-1, keepdims=True)
    inner = inner / enc
    own = own / enc + EPS
    other = other / enc + EPS
    inverse = lax.rsqrt(own * other)
    cosine = inner * inverse
    kept = keep_ref[...] * (-COEF / enc)
    left = kept * inverse
    right = kept * (cosine / own)
    for piece in range(pieces):
        cols = slice(piece * 384, (piece + 1) * 384)
        tgt = tea[:, :, cols].reshape(TOK, 384).astype(F32)
        gal[:, cols] = (tgt * left - right * aligned[:, cols]).astype(BF)

    @pl.loop(0, nz // 2)
    def _(step):
        pair = lax.rem(z // 2 + step, nz // 2)
        weights = wf[pl.ds(pair * 2, 2)].reshape(2 * HD, enc)
        back = lax.dot_general(gal[...], weights, NT, preferred_element_type=F32).astype(BF)
        for part in range(2):
            there = pair * 2 + part
            gsend[there] = back[:, part * HD:(part + 1) * HD]
            src = gsend.at[there]
            dst = gh.at[pl.ds(al(z * TOK, TOK), TOK)]

            @pl.when(there == z)
            def _():
                pltpu.make_async_copy(src, dst, mid_recv.at[1]).start()

            @pl.when(there != z)
            def _():
                remote(src, dst, mid_send.at[1], mid_recv.at[1], on_ring(2 * there + c)).start()

    waiting(gh, mid_recv.at[1])

    my_cols = pl.ds(al(z * HD, HD), HD)

    def send_out(src_ref, out_ref, a, s):
        src = src_ref.at[pl.ds(al(s * SEG, SEG), SEG)]
        dst = out_ref.at[c, :, my_cols]

        @pl.when(s == me)
        def _():
            pltpu.make_async_copy(src, dst, out_recv.at[a]).start()

        @pl.when(s != me)
        def _():
            remote(src, dst, out_send.at[a], out_recv.at[a], on_ring(s)).start()

    segs = bq // SEG

    @pl.loop(0, nb)
    def _(step):
        block = lax.rem(first + step, nb)
        span = pl.ds(al(block * bq, bq), bq)
        grad = gh[span].astype(F32) * linv[span]
        grad_b = grad.astype(BF)
        delta = jnp.sum(grad_b.astype(F32) * att_f[span], axis=-1, keepdims=True)
        raised = expo[span]
        grad_p = lax.dot_general(grad_b, va[:, :HD], NT, preferred_element_type=F32)
        grad_s = (raised.astype(F32) * (grad_p - delta)).astype(BF)
        acc_v[...] += jnp.dot(grad.T.astype(BF), raised, preferred_element_type=F32)
        acc_k[...] += jnp.dot(qh[span].astype(F32).T.astype(BF), grad_s, preferred_element_type=F32)
        grad_q = jnp.dot(grad_s, kh[...], preferred_element_type=F32)
        gq_h[span] = (grad_q * scale).astype(BF)
        for part in range(segs):
            send_out(gq_h, oq_ref, 0, block * segs + part)

    gv_h[...] = acc_v[...].T.astype(BF)

    @pl.loop(0, ns)
    def _(step):
        send_out(gv_h, ov_ref, 2, lax.rem(me + step, ns))

    gk_h[...] = (acc_k[...] * scale).T.astype(BF)

    @pl.loop(0, ns)
    def _(step):
        send_out(gk_h, ok_ref, 1, lax.rem(me + step, ns))

    waiting(tea, t_send)
    waiting(wf.at[pl.ds(0, nz - 1), c, band, :, wcols], w_send.at[0])
    waiting(wf.at[pl.ds(0, nr - 1), c], w_send.at[1])
    waiting(wf.at[:, c], w_send.at[2])
    most = pl.ds(0, total - SEG)
    for a, buf in enumerate((kh.at[most], qh.at[most], va.at[most, pl.ds(0, HD)])):
        waiting(buf, in_send.at[a])
    waiting(att_h.at[pl.ds(0, total - TOK)], mid_send.at[0])
    waiting(gsend.at[pl.ds(0, nz - 1)], mid_send.at[1])
    for a, buf in enumerate((gq_h, gk_h, gv_h)):
        waiting(buf.at[most], out_send.at[a])
    for a, buf in enumerate((oq_ref, ok_ref, ov_ref)):
        waiting(buf, out_recv.at[a])


def shards(queries, key_states, value_states, projector, teacher, enc_gain, enc_bias, valid_len):
    ns = lax.axis_size("seq")
    nz = ns // 2
    ndp = lax.axis_size("dp")
    nr = ndp * lax.axis_size("grp")
    count, seg, width = queries.shape
    enc = teacher.shape[-1]
    total = ns * seg
    bq = min(256, total // 2)
    me = lax.axis_index("seq")
    image = (lax.axis_index("grp") * ndp + lax.axis_index("dp")) * count + lax.rem(me, 2)
    length = lax.dynamic_slice_in_dim(valid_len, image, 1)
    key_bias = jnp.where(lax.iota(jnp.int32, total) < length, 0.0, -1e30).astype(F32)[None, :]
    token = (me // 2) * TOK + lax.iota(jnp.int32, TOK)
    keep = (token < length).astype(F32)[:, None]
    vm = pl.BlockSpec(memory_space=pltpu.VMEM)
    hbm = pl.BlockSpec(memory_space=pl.ANY)
    dma = pltpu.SemaphoreType.DMA
    head = pltpu.VMEM((total, HD), BF)
    head_f = pltpu.VMEM((total, HD), F32)
    out = jax.ShapeDtypeStruct(queries.shape, BF)
    return pl.pallas_call(
        functools.partial(kernel, nz, nr, ndp, bq),
        out_shape=[out, out, out],
        in_specs=[hbm, hbm, hbm, hbm, hbm, vm, vm, vm, vm],
        out_specs=[hbm, hbm, hbm],
        scratch_shapes=[
            head,
            head,
            pltpu.VMEM((total, 2 * HD), BF),
            pltpu.VMEM((nz, 2, 4, seg // 4, enc), BF),
            pltpu.VMEM((2, seg, enc), BF),
            head,
            pltpu.VMEM((TOK, width), BF),
            pltpu.VMEM((nz, TOK, HD), BF),
            head,
            head,
            head,
            head,
            pltpu.VMEM((total, total), BF),
            head_f,
            head_f,
            pltpu.VMEM((TOK, enc), F32),
            pltpu.VMEM((TOK, enc), BF),
            pltpu.VMEM((HD, total), F32),
            pltpu.VMEM((HD, total), F32),
            dma((3,)),
            dma((3,)),
            dma((3,)),
            dma((3,)),
            dma,
            dma,
            dma((2,)),
            dma((2,)),
            dma((3,)),
            dma((3,)),
        ],
        compiler_params=pltpu.CompilerParams(
            collective_id=0, has_side_effects=True, vmem_limit_bytes=58 << 20
        ),
    )(
        queries,
        key_states,
        value_states,
        projector.reshape(4, seg // 4, enc),
        teacher,
        enc_gain[None, :],
        enc_bias[None, :],
        key_bias,
        keep,
    )


def solution(mesh):
    rows = P(("grp", "dp"), "seq", None)
    return jax.shard_map(
        shards,
        mesh=mesh,
        in_specs=(rows, rows, rows, P("seq", None), rows, P(), P(), P()),
        out_specs=(rows, rows, rows),
        check_vma=False,
    )
```

```python
import functools

import jax
import jax.numpy as jnp
from jax import lax
from jax.experimental import pallas as pl
from jax.experimental.pallas import tpu as pltpu
from jax.sharding import PartitionSpec as P

HD = 128
SEG = 64
TOK = 2 * SEG
EPS = 1e-06
COEF = 2048.0
LOG2E = 1.4426950408889634
MESH = pl.DeviceIdType.MESH
BF = jnp.bfloat16
F32 = jnp.float32
NT = (((1,), (1,)), ((), ()))


def al(value, step):
    return pl.multiple_of(value, step)


def kernel(
    nz, nr, ndp, bq,
    q_ref, k_ref, v_ref, w_ref, t_ref, gain_ref, bias_ref, len_ref,
    oq_ref, ok_ref, ov_ref,
    stage, t_stage, kb_ref, qh, kh, va, wf, tea, att_h, rows, gsend, gh, gq_h, gk_h, gv_h,
    expo, att_f, linv, aligned, gal, acc_k, acc_v,
    st_send, st_recv, in_send, in_recv, w_send, w_recv, t_send, t_recv, mid_send, mid_recv, out_send, out_recv,
):
    ns = 2 * nz
    total = ns * SEG
    enc = t_ref.shape[-1]
    cq = nr // 4
    cw = enc // cq
    nb = total // bq
    per = bq // TOK
    tq = min(4, nr // 2)
    tc = nr // (2 * tq)
    scale = HD ** (-0.5)

    me = lax.axis_index("seq")
    ring = lax.axis_index("grp") * ndp + lax.axis_index("dp")
    z = me // 2
    c = lax.rem(me, 2)

    def on_ring(s):
        return {"seq": s}

    def in_plane(r):
        return {"grp": r // ndp, "dp": lax.rem(r, ndp)}

    def at(r, s):
        return {"grp": r // ndp, "dp": lax.rem(r, ndp), "seq": s}

    barrier = pltpu.get_barrier_semaphore()

    def greet(device):
        pl.semaphore_signal(barrier, 1, device_id=device, device_id_type=MESH)

    @pl.loop(1, ns)
    def _(step):
        greet(on_ring(lax.rem(me + step, ns)))

    @pl.loop(1, nr)
    def _(step):
        greet(in_plane(lax.rem(ring + step, nr)))

    @pl.loop(0, nr)
    def _(step):
        head = lax.rem(ring + step, nr)
        for core in range(2):
            @pl.when((head != ring) & (2 * ring + core != me))
            def _():
                greet(at(head, 2 * ring + core))

    @pl.when(ring == z)
    def _():
        pl.semaphore_wait(barrier, ns - 1 + nr - 1)

    @pl.when(ring != z)
    def _():
        pl.semaphore_wait(barrier, 2 * (ns - 1) + nr - 1)

    def remote(src, dst, ssem, rsem, device):
        return pltpu.make_async_remote_copy(
            src_ref=src, dst_ref=dst, send_sem=ssem, recv_sem=rsem, device_id=device, device_id_type=MESH
        )

    def waiting(view, sem):
        pltpu.make_async_copy(view, view, sem).wait()

    band = ring // cq
    wcols = pl.ds(al(lax.rem(ring, cq) * cw, 128), cw)
    own_w = w_ref.at[band, :, wcols]

    @pl.loop(1, nz)
    def _(step):
        there = lax.rem(z + step, nz)
        remote(
            own_w, wf.at[z, c, band, :, wcols], w_send.at[0], w_recv.at[0], on_ring(2 * there + c)
        ).start()

    pltpu.make_async_copy(own_w, wf.at[z, c, band, :, wcols], w_recv.at[0]).start()

    mine = pl.ds(al(me * SEG, SEG), SEG)
    sources = (k_ref, q_ref, v_ref)
    places = (kh.at[mine], qh.at[mine], va.at[mine, pl.ds(0, HD)])

    def scatter_inputs(image):
        for a in range(3):
            @pl.loop(1, nr)
            def _(step):
                head = lax.rem(ring + step, nr)
                remote(
                    sources[a].at[image, :, pl.ds(al(head * HD, HD), HD)], stage.at[image, a, ring],
                    st_send.at[image, a], st_recv.at[image, a], in_plane(head),
                ).start()

            pltpu.make_async_copy(
                sources[a].at[image, :, pl.ds(al(ring * HD, HD), HD)], stage.at[image, a, ring],
                st_recv.at[image, a],
            ).start()

    def pass_inputs(image):
        for a in range(3):
            waiting(stage.at[image, a], st_recv.at[image, a])

            @pl.loop(1, nz)
            def _(step):
                plane = lax.rem(z + step, nz)
                remote(
                    stage.at[image, a, plane], places[a], in_send.at[a], in_recv.at[a],
                    on_ring(2 * plane + image),
                ).start()

            @pl.when(c == image)
            def _():
                pltpu.make_async_copy(stage.at[image, a, z], places[a], in_recv.at[a]).start()

            @pl.when(c != image)
            def _():
                remote(
                    stage.at[image, a, z], places[a], in_send.at[a], in_recv.at[a], on_ring(2 * z + image)
                ).start()

    t_rows = SEG // tq
    t_cols = enc // tc

    def part_of(p):
        rest = lax.rem(p, tq * tc)
        return (
            p // (tq * tc),
            pl.ds(al(rest // tc * t_rows, t_rows), t_rows),
            pl.ds(al(lax.rem(rest, tc) * t_cols, 128), t_cols),
        )

    def scatter_teacher():
        @pl.loop(1, nr)
        def _(step):
            by = lax.rem(ring + step, nr)
            image, rows_at, cols_at = part_of(by)
            remote(
                t_ref.at[image, rows_at, cols_at], t_stage.at[ring], t_send.at[0], t_recv.at[0], in_plane(by)
            ).start()

        image, rows_at, cols_at = part_of(ring)
        pltpu.make_async_copy(t_ref.at[image, rows_at, cols_at], t_stage.at[ring], t_recv.at[0]).start()

    t_image, t_rows_at, t_cols_at = part_of(ring)

    def pass_teacher():
        waiting(t_stage, t_recv.at[0])

        @pl.loop(0, nr)
        def _(step):
            origin = lax.rem(z + nr // 2 + step, nr)
            plane = lax.rem(origin + nr // 2, nr)
            src = t_stage.at[origin]
            dst = tea.at[c, t_rows_at, t_cols_at]
            here = (ring == z) & (plane == z) & (t_image == c)

            @pl.when(here)
            def _():
                pltpu.make_async_copy(src, dst, t_recv.at[1]).start()

            @pl.when(jnp.logical_not(here))
            def _():
                remote(src, dst, t_send.at[1], t_recv.at[1], at(z, 2 * plane + t_image)).start()

    scatter_inputs(0)
    scatter_teacher()
    scatter_inputs(1)
    pass_inputs(0)

    @pl.when(t_image == 0)
    def _():
        pass_teacher()

    part_w = wf.at[:, c, band, :, wcols]
    waiting(part_w, w_recv.at[0])

    @pl.loop(1, nr)
    def _(step):
        remote(
            part_w, part_w, w_send.at[1], w_recv.at[1], in_plane(lax.rem(ring + step, nr))
        ).start()

    pass_inputs(1)

    @pl.when(t_image == 1)
    def _():
        pass_teacher()

    length = len_ref[2 * z + c]
    keys_at = lax.broadcasted_iota(jnp.int32, (1, total), 1)
    kb_ref[...] = jnp.where(keys_at < length, 0.0, -1e30).astype(F32)
    va[:, HD:] = jnp.ones((total, HD), BF)
    acc_k[...] = jnp.zeros_like(acc_k)
    acc_v[...] = jnp.zeros_like(acc_v)

    def swap_w():
        waiting(wf.at[pl.ds(0, nr - 1), c], w_recv.at[1])
        half = wf.at[:, c]
        remote(half, half, w_send.at[2], w_recv.at[2], on_ring(2 * z + 1 - c)).start()

    @pl.when(c == 1)
    def _():
        swap_w()

    waiting(kh, in_recv.at[0])
    waiting(qh, in_recv.at[1])
    waiting(va.at[:, pl.ds(0, HD)], in_recv.at[2])

    first = ring // per

    @pl.loop(0, nb)
    def _(step):
        block = lax.rem(first + step, nb)
        span = pl.ds(al(block * bq, bq), bq)
        scores = lax.dot_general(qh[span], kh[...], NT, preferred_element_type=F32)
        scores = scores * (scale * LOG2E) + kb_ref[...]
        top = jnp.max(scores, axis=-1, keepdims=True)
        raised = jnp.exp2(scores - top).astype(BF)
        expo[span] = raised
        both = jnp.dot(raised, va[...], preferred_element_type=F32)
        inverse = 1.0 / both[:, HD:]
        attended = both[:, :HD] * inverse
        linv[span] = inverse
        att_f[span] = attended
        att_h[span] = attended.astype(BF)
        for part in range(per):
            there = block * per + part
            src = att_h.at[pl.ds(al(there * TOK, TOK), TOK)]
            dst = rows.at[:, pl.ds(al(ring * HD, HD), HD)]

            @pl.when(there == ring)
            def _():
                pltpu.make_async_copy(src, dst, mid_recv.at[0]).start()

            @pl.when(there != ring)
            def _():
                remote(src, dst, mid_send.at[0], mid_recv.at[0], in_plane(there)).start()

    @pl.when(c == 0)
    def _():
        swap_w()

    waiting(tea, t_recv.at[1])
    for seg in range(2):
        data = tea[seg].astype(F32)
        center = data - jnp.mean(data, axis=-1, keepdims=True)
        spread = jnp.mean(center * center, axis=-1, keepdims=True)
        tea[seg] = (center * lax.rsqrt(spread + EPS) * gain_ref[...][None, :] + bias_ref[...][None, :]).astype(BF)

    waiting(rows, mid_recv.at[0])
    waiting(wf.at[:, 1 - c], w_recv.at[2])

    pieces = enc // 384
    inner = jnp.zeros((TOK, 1), F32)
    own = jnp.zeros((TOK, 1), F32)
    other = jnp.zeros((TOK, 1), F32)
    for piece in range(pieces):
        cols = slice(piece * 384, (piece + 1) * 384)
        weights = wf[:, :, :, :, cols].reshape(nz * HD, 384)
        out = jnp.dot(rows[...], weights, preferred_element_type=F32)
        aligned[:, cols] = out
        tgt = tea[:, :, cols].reshape(TOK, 384).astype(F32)
        inner += jnp.sum(out * tgt, axis=-1, keepdims=True)
        own += jnp.sum(out * out, axis=-1, keepdims=True)
        other += jnp.sum(tgt * tgt, axis=-1, keepdims=True)
    inner = inner / enc
    own = own / enc + EPS
    other = other / enc + EPS
    inverse = lax.rsqrt(own * other)
    cosine = inner * inverse
    token = ring * TOK + lax.broadcasted_iota(jnp.int32, (TOK, 1), 0)
    kept = jnp.where(token < length, -COEF / enc, 0.0).astype(F32)
    left = kept * inverse
    right = kept * (cosine / own)
    for piece in range(pieces):
        cols = slice(piece * 384, (piece + 1) * 384)
        tgt = tea[:, :, cols].reshape(TOK, 384).astype(F32)
        gal[:, cols] = (tgt * left - right * aligned[:, cols]).astype(BF)

    @pl.loop(0, nz // 2)
    def _(step):
        pair = lax.rem(ring // 2 + step, nz // 2)
        weights = wf[pl.ds(pair * 2, 2)].reshape(2 * HD, enc)
        back = lax.dot_general(gal[...], weights, NT, preferred_element_type=F32).astype(BF)
        for part in range(2):
            there = pair * 2 + part
            gsend[there] = back[:, part * HD:(part + 1) * HD]
            src = gsend.at[there]
            dst = gh.at[pl.ds(al(ring * TOK, TOK), TOK)]

            @pl.when(there == ring)
            def _():
                pltpu.make_async_copy(src, dst, mid_recv.at[1]).start()

            @pl.when(there != ring)
            def _():
                remote(src, dst, mid_send.at[1], mid_recv.at[1], in_plane(there)).start()

    waiting(gh, mid_recv.at[1])

    my_cols = pl.ds(al(ring * HD, HD), HD)

    def send_out(src_ref, out_ref, a, s):
        src = src_ref.at[pl.ds(al(s * SEG, SEG), SEG)]
        dst = out_ref.at[c, :, my_cols]

        here = (s == me) & (ring == z)

        @pl.when(here)
        def _():
            pltpu.make_async_copy(src, dst, out_recv.at[a]).start()

        @pl.when(jnp.logical_not(here))
        def _():
            remote(src, dst, out_send.at[a], out_recv.at[a], at(z, s)).start()

    segs = bq // SEG

    @pl.loop(0, nb)
    def _(step):
        block = lax.rem(first + step, nb)
        span = pl.ds(al(block * bq, bq), bq)
        grad = gh[span].astype(F32) * linv[span]
        grad_b = grad.astype(BF)
        delta = jnp.sum(grad_b.astype(F32) * att_f[span], axis=-1, keepdims=True)
        raised = expo[span]
        grad_p = lax.dot_general(grad_b, va[:, :HD], NT, preferred_element_type=F32)
        grad_s = (raised.astype(F32) * (grad_p - delta)).astype(BF)
        acc_v[...] += jnp.dot(grad.T.astype(BF), raised, preferred_element_type=F32)
        acc_k[...] += jnp.dot(qh[span].astype(F32).T.astype(BF), grad_s, preferred_element_type=F32)
        grad_q = jnp.dot(grad_s, kh[...], preferred_element_type=F32)
        gq_h[span] = (grad_q * scale).astype(BF)
        for part in range(segs):
            send_out(gq_h, oq_ref, 0, block * segs + part)

    gv_h[...] = acc_v[...].T.astype(BF)

    @pl.loop(0, ns)
    def _(step):
        send_out(gv_h, ov_ref, 2, lax.rem(me + step, ns))

    gk_h[...] = (acc_k[...] * scale).T.astype(BF)

    @pl.loop(0, ns)
    def _(step):
        send_out(gk_h, ok_ref, 1, lax.rem(me + step, ns))

    waiting(wf.at[pl.ds(0, nz - 1), c, band, :, wcols], w_send.at[0])
    waiting(wf.at[pl.ds(0, nr - 1), c], w_send.at[1])
    waiting(wf.at[:, c], w_send.at[2])
    others = pl.ds(0, nr - 1)
    waiting(t_stage.at[others], t_send.at[0])
    t_here = (ring == z) & (t_image == c)

    @pl.when(t_here)
    def _():
        waiting(t_stage.at[others], t_send.at[1])

    @pl.when(jnp.logical_not(t_here))
    def _():
        waiting(t_stage, t_send.at[1])

    for image in range(2):
        for a in range(3):
            waiting(stage.at[image, a, others], st_send.at[image, a])
    most = pl.ds(0, total - SEG)
    for a, buf in enumerate((kh.at[most], qh.at[most], va.at[most, pl.ds(0, HD)])):
        waiting(buf, in_send.at[a])
    waiting(att_h.at[pl.ds(0, total - TOK)], mid_send.at[0])
    waiting(gsend.at[others], mid_send.at[1])
    for a, buf in enumerate((gq_h, gk_h, gv_h)):
        @pl.when(ring == z)
        def _():
            waiting(buf.at[most], out_send.at[a])

        @pl.when(ring != z)
        def _():
            waiting(buf, out_send.at[a])

    for a, buf in enumerate((oq_ref, ok_ref, ov_ref)):
        waiting(buf, out_recv.at[a])


def shards(queries, key_states, value_states, projector, teacher, enc_gain, enc_bias, valid_len):
    ns = lax.axis_size("seq")
    nz = ns // 2
    ndp = lax.axis_size("dp")
    nr = ndp * lax.axis_size("grp")
    count, seg, width = queries.shape
    enc = teacher.shape[-1]
    total = ns * seg
    bq = min(256, total // 2)
    tq = min(4, nr // 2)
    tc = nr // (2 * tq)
    vm = pl.BlockSpec(memory_space=pltpu.VMEM)
    hbm = pl.BlockSpec(memory_space=pl.ANY)
    dma = pltpu.SemaphoreType.DMA
    head = pltpu.VMEM((total, HD), BF)
    head_f = pltpu.VMEM((total, HD), F32)
    out = jax.ShapeDtypeStruct(queries.shape, BF)
    return pl.pallas_call(
        functools.partial(kernel, nz, nr, ndp, bq),
        out_shape=[out, out, out],
        in_specs=[hbm, hbm, hbm, hbm, hbm, vm, vm, pl.BlockSpec(memory_space=pltpu.SMEM)],
        out_specs=[hbm, hbm, hbm],
        scratch_shapes=[
            pltpu.VMEM((2, 3, nr, seg, HD), BF),
            pltpu.VMEM((nr, seg // tq, enc // tc), BF),
            pltpu.VMEM((1, total), F32),
            head,
            head,
            pltpu.VMEM((total, 2 * HD), BF),
            pltpu.VMEM((nz, 2, 4, seg // 4, enc), BF),
            pltpu.VMEM((2, seg, enc), BF),
            head,
            pltpu.VMEM((TOK, width), BF),
            pltpu.VMEM((nz, TOK, HD), BF),
            head,
            head,
            head,
            head,
            pltpu.VMEM((total, total), BF),
            head_f,
            head_f,
            pltpu.VMEM((TOK, enc), F32),
            pltpu.VMEM((TOK, enc), BF),
            pltpu.VMEM((HD, total), F32),
            pltpu.VMEM((HD, total), F32),
            dma((2, 3)),
            dma((2, 3)),
            dma((3,)),
            dma((3,)),
            dma((3,)),
            dma((3,)),
            dma((2,)),
            dma((2,)),
            dma((2,)),
            dma((2,)),
            dma((3,)),
            dma((3,)),
        ],
        compiler_params=pltpu.CompilerParams(
            collective_id=0, has_side_effects=True, vmem_limit_bytes=58 << 20
        ),
    )(
        queries,
        key_states,
        value_states,
        projector.reshape(4, seg // 4, enc),
        teacher,
        enc_gain,
        enc_bias,
        valid_len,
    )


def solution(mesh):
    rows = P(("grp", "dp"), "seq", None)
    return jax.shard_map(
        shards,
        mesh=mesh,
        in_specs=(rows, rows, rows, P("seq", None), rows, P(), P(), P()),
        out_specs=(rows, rows, rows),
        check_vma=False,
    )
```

```python
import functools

import jax
import jax.numpy as jnp
from jax import lax
from jax.experimental import pallas as pl
from jax.experimental.pallas import tpu as pltpu
from jax.sharding import PartitionSpec as P

HD = 128
SEG = 64
TOK = 2 * SEG
EPS = 1e-06
COEF = 2048.0
LOG2E = 1.4426950408889634
MESH = pl.DeviceIdType.MESH
BF = jnp.bfloat16
F32 = jnp.float32
NT = (((1,), (1,)), ((), ()))


def al(value, step):
    return pl.multiple_of(value, step)


def kernel(
    nz, nr, ndp, bq,
    q_ref, k_ref, v_ref, w_ref, t_ref, gain_ref, bias_ref, len_ref,
    oq_ref, ok_ref, ov_ref,
    stage, t_stage, kb_ref, qh, kh, va, wf, tea, att_h, rows, gsend, gh, gq_h, gk_h, gv_h,
    expo, att_f, linv, aligned, gal, acc_q, grad_t, q_t, delta,
    st_send, st_recv, in_send, in_recv, w_send, w_recv, t_send, t_recv, mid_send, mid_recv, out_send, out_recv,
):
    ns = 2 * nz
    total = ns * SEG
    enc = t_ref.shape[-1]
    cq = nr // 4
    cw = enc // cq
    nb = total // bq
    per = bq // TOK
    tq = min(4, nr // 2)
    tc = nr // (2 * tq)
    scale = HD ** (-0.5)

    me = lax.axis_index("seq")
    ring = lax.axis_index("grp") * ndp + lax.axis_index("dp")
    z = me // 2
    c = lax.rem(me, 2)

    def on_ring(s):
        return {"seq": s}

    def in_plane(r):
        return {"grp": r // ndp, "dp": lax.rem(r, ndp)}

    def at(r, s):
        return {"grp": r // ndp, "dp": lax.rem(r, ndp), "seq": s}

    barrier = pltpu.get_barrier_semaphore()

    def greet(device):
        pl.semaphore_signal(barrier, 1, device_id=device, device_id_type=MESH)

    @pl.loop(1, ns)
    def _(step):
        greet(on_ring(lax.rem(me + step, ns)))

    @pl.loop(1, nr)
    def _(step):
        greet(in_plane(lax.rem(ring + step, nr)))

    @pl.loop(0, nr)
    def _(step):
        head = lax.rem(ring + step, nr)
        for core in range(2):
            @pl.when((head != ring) & (2 * ring + core != me))
            def _():
                greet(at(head, 2 * ring + core))

    @pl.when(ring == z)
    def _():
        pl.semaphore_wait(barrier, ns - 1 + nr - 1)

    @pl.when(ring != z)
    def _():
        pl.semaphore_wait(barrier, 2 * (ns - 1) + nr - 1)

    def remote(src, dst, ssem, rsem, device):
        return pltpu.make_async_remote_copy(
            src_ref=src, dst_ref=dst, send_sem=ssem, recv_sem=rsem, device_id=device, device_id_type=MESH
        )

    def waiting(view, sem):
        pltpu.make_async_copy(view, view, sem).wait()

    band = ring // cq
    wcols = pl.ds(al(lax.rem(ring, cq) * cw, 128), cw)
    own_w = w_ref.at[band, :, wcols]

    own_place = wf.at[z // 4, lax.rem(z, 4), c, band, :, wcols]

    @pl.loop(1, nz // 4)
    def _(step):
        there = lax.rem(z + 4 * step, nz)
        remote(own_w, own_place, w_send.at[0], w_recv.at[0], on_ring(2 * there + c)).start()

    pltpu.make_async_copy(own_w, own_place, w_recv.at[0]).start()

    def pass_w():
        class_w = wf.at[:, lax.rem(z, 4), c, band, :, wcols]
        waiting(class_w, w_recv.at[0])
        for apart in (1, nz - 1, 2):
            there = lax.rem(z + apart, nz)
            remote(class_w, class_w, w_send.at[3], w_recv.at[3], on_ring(2 * there + c)).start()

    mine = pl.ds(al(me * SEG, SEG), SEG)
    sources = (k_ref, q_ref, v_ref)
    places = (kh.at[mine], qh.at[mine], va.at[mine, pl.ds(0, HD)])

    def scatter_inputs(image):
        for a in range(3):
            @pl.loop(1, nr)
            def _(step):
                head = lax.rem(ring + step, nr)
                remote(
                    sources[a].at[image, :, pl.ds(al(head * HD, HD), HD)], stage.at[image, a, ring],
                    st_send.at[image, a], st_recv.at[image, a], in_plane(head),
                ).start()

            pltpu.make_async_copy(
                sources[a].at[image, :, pl.ds(al(ring * HD, HD), HD)], stage.at[image, a, ring],
                st_recv.at[image, a],
            ).start()

    def pass_inputs(image):
        for a in range(3):
            waiting(stage.at[image, a], st_recv.at[image, a])

            @pl.loop(1, nz)
            def _(step):
                plane = lax.rem(z + step, nz)
                remote(
                    stage.at[image, a, plane], places[a], in_send.at[a], in_recv.at[a],
                    on_ring(2 * plane + image),
                ).start()

            @pl.when(c == image)
            def _():
                pltpu.make_async_copy(stage.at[image, a, z], places[a], in_recv.at[a]).start()

            @pl.when(c != image)
            def _():
                remote(
                    stage.at[image, a, z], places[a], in_send.at[a], in_recv.at[a], on_ring(2 * z + image)
                ).start()

    t_rows = SEG // tq
    t_cols = enc // tc

    def part_of(p):
        rest = lax.rem(p, tq * tc)
        return (
            p // (tq * tc),
            pl.ds(al(rest // tc * t_rows, t_rows), t_rows),
            pl.ds(al(lax.rem(rest, tc) * t_cols, 128), t_cols),
        )

    def scatter_teacher():
        @pl.loop(1, nr)
        def _(step):
            by = lax.rem(ring + step, nr)
            image, rows_at, cols_at = part_of(by)
            remote(
                t_ref.at[image, rows_at, cols_at], t_stage.at[ring], t_send.at[0], t_recv.at[0], in_plane(by)
            ).start()

        image, rows_at, cols_at = part_of(ring)
        pltpu.make_async_copy(t_ref.at[image, rows_at, cols_at], t_stage.at[ring], t_recv.at[0]).start()

    t_image, t_rows_at, t_cols_at = part_of(ring)

    def pass_teacher():
        waiting(t_stage, t_recv.at[0])

        @pl.loop(0, nr)
        def _(step):
            origin = lax.rem(z + nr // 2 + step, nr)
            plane = lax.rem(origin + nr // 2, nr)
            src = t_stage.at[origin]
            dst = tea.at[c, t_rows_at, t_cols_at]
            here = (ring == z) & (plane == z) & (t_image == c)

            @pl.when(here)
            def _():
                pltpu.make_async_copy(src, dst, t_recv.at[1]).start()

            @pl.when(jnp.logical_not(here))
            def _():
                remote(src, dst, t_send.at[1], t_recv.at[1], at(z, 2 * plane + t_image)).start()

    scatter_inputs(0)
    scatter_teacher()
    scatter_inputs(1)
    pass_w()
    pass_inputs(0)

    @pl.when(t_image == 0)
    def _():
        pass_teacher()

    part_w = wf.at[:, :, c, band, :, wcols]
    waiting(wf.at[:, pl.ds(0, 3), c, band, :, wcols], w_recv.at[3])

    @pl.loop(1, nr)
    def _(step):
        remote(
            part_w, part_w, w_send.at[1], w_recv.at[1], in_plane(lax.rem(ring + step, nr))
        ).start()

    pass_inputs(1)

    @pl.when(t_image == 1)
    def _():
        pass_teacher()

    length = len_ref[2 * z + c]
    keys_at = lax.broadcasted_iota(jnp.int32, (1, total), 1)
    kb_ref[...] = jnp.where(keys_at < length, 0.0, -1e30).astype(F32)
    va[:, HD:] = jnp.ones((total, HD), BF)
    acc_q[...] = jnp.zeros_like(acc_q)

    most_w = expo.at[pl.ds(0, (nr - 1) * nz * (SEG // 4) * cw // total)]

    def swap_w():
        waiting(most_w, w_recv.at[1])
        half = wf.at[:, :, c]
        remote(half, half, w_send.at[2], w_recv.at[2], on_ring(2 * z + 1 - c)).start()

    @pl.when(c == 1)
    def _():
        swap_w()

    waiting(kh, in_recv.at[0])
    waiting(qh, in_recv.at[1])
    waiting(va.at[:, pl.ds(0, HD)], in_recv.at[2])

    first = ring // per

    @pl.loop(0, nb)
    def _(step):
        block = lax.rem(first + step, nb)
        span = pl.ds(al(block * bq, bq), bq)
        scores = lax.dot_general(qh[span], kh[...], NT, preferred_element_type=F32)
        scores = scores * (scale * LOG2E) + kb_ref[...]
        top = jnp.max(scores, axis=-1, keepdims=True)
        raised = jnp.exp2(scores - top).astype(BF)
        expo[span] = raised
        both = jnp.dot(raised, va[...], preferred_element_type=F32)
        inverse = 1.0 / both[:, HD:]
        attended = both[:, :HD] * inverse
        linv[span] = inverse
        att_f[span] = attended
        att_h[span] = attended.astype(BF)
        for part in range(per):
            there = block * per + part
            src = att_h.at[pl.ds(al(there * TOK, TOK), TOK)]
            dst = rows.at[:, pl.ds(al(ring * HD, HD), HD)]

            @pl.when(there == ring)
            def _():
                pltpu.make_async_copy(src, dst, mid_recv.at[0]).start()

            @pl.when(there != ring)
            def _():
                remote(src, dst, mid_send.at[0], mid_recv.at[0], in_plane(there)).start()

    @pl.when(c == 0)
    def _():
        swap_w()

    waiting(tea, t_recv.at[1])
    for seg in range(2):
        data = tea[seg].astype(F32)
        center = data - jnp.mean(data, axis=-1, keepdims=True)
        spread = jnp.mean(center * center, axis=-1, keepdims=True)
        tea[seg] = (center * lax.rsqrt(spread + EPS) * gain_ref[...][None, :] + bias_ref[...][None, :]).astype(BF)

    waiting(rows, mid_recv.at[0])
    waiting(wf.at[:, :, 1 - c], w_recv.at[2])

    pieces = enc // 384
    inner = jnp.zeros((TOK, 1), F32)
    own = jnp.zeros((TOK, 1), F32)
    other = jnp.zeros((TOK, 1), F32)
    for piece in range(pieces):
        cols = slice(piece * 384, (piece + 1) * 384)
        weights = wf[:, :, :, :, :, cols].reshape(nz * HD, 384)
        out = jnp.dot(rows[...], weights, preferred_element_type=F32)
        aligned[:, cols] = out
        tgt = tea[:, :, cols].reshape(TOK, 384).astype(F32)
        inner += jnp.sum(out * tgt, axis=-1, keepdims=True)
        own += jnp.sum(out * out, axis=-1, keepdims=True)
        other += jnp.sum(tgt * tgt, axis=-1, keepdims=True)
    inner = inner / enc
    own = own / enc + EPS
    other = other / enc + EPS
    inverse = lax.rsqrt(own * other)
    cosine = inner * inverse
    token = ring * TOK + lax.broadcasted_iota(jnp.int32, (TOK, 1), 0)
    kept = jnp.where(token < length, -COEF / enc, 0.0).astype(F32)
    left = kept * inverse
    right = kept * (cosine / own)
    for piece in range(pieces):
        cols = slice(piece * 384, (piece + 1) * 384)
        tgt = tea[:, :, cols].reshape(TOK, 384).astype(F32)
        gal[:, cols] = (tgt * left - right * aligned[:, cols]).astype(BF)

    @pl.loop(0, nz // 2)
    def _(step):
        pair = lax.rem(ring // 2 + step, nz // 2)
        weights = wf[pair // 2, pl.ds(lax.rem(pair, 2) * 2, 2)].reshape(2 * HD, enc)
        back = lax.dot_general(gal[...], weights, NT, preferred_element_type=F32).astype(BF)
        for part in range(2):
            there = pair * 2 + part
            gsend[there] = back[:, part * HD:(part + 1) * HD]
            src = gsend.at[there]
            dst = gh.at[pl.ds(al(ring * TOK, TOK), TOK)]

            @pl.when(there == ring)
            def _():
                pltpu.make_async_copy(src, dst, mid_recv.at[1]).start()

            @pl.when(there != ring)
            def _():
                remote(src, dst, mid_send.at[1], mid_recv.at[1], in_plane(there)).start()

    waiting(gh, mid_recv.at[1])

    my_cols = pl.ds(al(ring * HD, HD), HD)

    def send_out(src_ref, out_ref, a, s):
        src = src_ref.at[pl.ds(al(s * SEG, SEG), SEG)]
        dst = out_ref.at[c, :, my_cols]

        here = (s == me) & (ring == z)

        @pl.when(here)
        def _():
            pltpu.make_async_copy(src, dst, out_recv.at[a]).start()

        @pl.when(jnp.logical_not(here))
        def _():
            remote(src, dst, out_send.at[a], out_recv.at[a], at(z, s)).start()

    segs = bq // SEG

    @pl.loop(0, nb)
    def _(block):
        span = pl.ds(al(block * bq, bq), bq)
        grad = gh[span].astype(F32) * linv[span]
        grad_b = grad.astype(BF)
        gh[span] = grad_b
        grad_t[:, span] = grad.T.astype(BF)
        q_t[:, span] = qh[span].astype(F32).T.astype(BF)
        delta[span] = jnp.sum(grad_b.astype(F32) * att_f[span], axis=-1, keepdims=True)

    @pl.loop(0, nb)
    def _(step):
        block = lax.rem(z // per + step, nb)
        span = pl.ds(al(block * bq, bq), bq)
        raised = expo[:, span]
        grad_v = jnp.dot(grad_t[...], raised, preferred_element_type=F32)
        gv_h[span] = grad_v.T.astype(BF)
        for part in range(segs):
            send_out(gv_h, ov_ref, 2, block * segs + part)
        grad_p = lax.dot_general(gh[...], va[span, :HD], NT, preferred_element_type=F32)
        grad_s = (raised.astype(F32) * (grad_p - delta[...])).astype(BF)
        grad_k = jnp.dot(q_t[...], grad_s, preferred_element_type=F32)
        gk_h[span] = (grad_k * scale).T.astype(BF)
        for part in range(segs):
            send_out(gk_h, ok_ref, 1, block * segs + part)
        acc_q[...] += jnp.dot(grad_s, kh[span], preferred_element_type=F32)

    gq_h[...] = (acc_q[...] * scale).astype(BF)

    @pl.loop(0, ns)
    def _(step):
        send_out(gq_h, oq_ref, 0, lax.rem(me + step, ns))

    if nz > 4:
        waiting(wf.at[pl.ds(0, nz // 4 - 1), 0, c, band, :, wcols], w_send.at[0])
    waiting(wf.at[:, pl.ds(0, 3), c, band, :, wcols], w_send.at[3])
    waiting(most_w, w_send.at[1])
    waiting(wf.at[:, :, c], w_send.at[2])
    others = pl.ds(0, nr - 1)
    waiting(t_stage.at[others], t_send.at[0])
    t_here = (ring == z) & (t_image == c)

    @pl.when(t_here)
    def _():
        waiting(t_stage.at[others], t_send.at[1])

    @pl.when(jnp.logical_not(t_here))
    def _():
        waiting(t_stage, t_send.at[1])

    for image in range(2):
        for a in range(3):
            waiting(stage.at[image, a, others], st_send.at[image, a])
    most = pl.ds(0, total - SEG)
    for a, buf in enumerate((kh.at[most], qh.at[most], va.at[most, pl.ds(0, HD)])):
        waiting(buf, in_send.at[a])
    waiting(att_h.at[pl.ds(0, total - TOK)], mid_send.at[0])
    waiting(gsend.at[others], mid_send.at[1])
    for a, buf in enumerate((gq_h, gk_h, gv_h)):
        @pl.when(ring == z)
        def _():
            waiting(buf.at[most], out_send.at[a])

        @pl.when(ring != z)
        def _():
            waiting(buf, out_send.at[a])

    for a, buf in enumerate((oq_ref, ok_ref, ov_ref)):
        waiting(buf, out_recv.at[a])


def shards(queries, key_states, value_states, projector, teacher, enc_gain, enc_bias, valid_len):
    ns = lax.axis_size("seq")
    nz = ns // 2
    ndp = lax.axis_size("dp")
    nr = ndp * lax.axis_size("grp")
    count, seg, width = queries.shape
    enc = teacher.shape[-1]
    total = ns * seg
    bq = min(256, total // 2)
    tq = min(4, nr // 2)
    tc = nr // (2 * tq)
    vm = pl.BlockSpec(memory_space=pltpu.VMEM)
    hbm = pl.BlockSpec(memory_space=pl.ANY)
    dma = pltpu.SemaphoreType.DMA
    head = pltpu.VMEM((total, HD), BF)
    head_f = pltpu.VMEM((total, HD), F32)
    out = jax.ShapeDtypeStruct(queries.shape, BF)
    return pl.pallas_call(
        functools.partial(kernel, nz, nr, ndp, bq),
        out_shape=[out, out, out],
        in_specs=[hbm, hbm, hbm, hbm, hbm, vm, vm, pl.BlockSpec(memory_space=pltpu.SMEM)],
        out_specs=[hbm, hbm, hbm],
        scratch_shapes=[
            pltpu.VMEM((2, 3, nr, seg, HD), BF),
            pltpu.VMEM((nr, seg // tq, enc // tc), BF),
            pltpu.VMEM((1, total), F32),
            head,
            head,
            pltpu.VMEM((total, 2 * HD), BF),
            pltpu.VMEM((nz // 4, 4, 2, 4, seg // 4, enc), BF),
            pltpu.VMEM((2, seg, enc), BF),
            head,
            pltpu.VMEM((TOK, width), BF),
            pltpu.VMEM((nz, TOK, HD), BF),
            head,
            head,
            head,
            head,
            pltpu.VMEM((total, total), BF),
            head_f,
            head_f,
            pltpu.VMEM((TOK, enc), F32),
            pltpu.VMEM((TOK, enc), BF),
            head_f,
            pltpu.VMEM((HD, total), BF),
            pltpu.VMEM((HD, total), BF),
            pltpu.VMEM((total, 1), F32),
            dma((2, 3)),
            dma((2, 3)),
            dma((3,)),
            dma((3,)),
            dma((4,)),
            dma((4,)),
            dma((2,)),
            dma((2,)),
            dma((2,)),
            dma((2,)),
            dma((3,)),
            dma((3,)),
        ],
        compiler_params=pltpu.CompilerParams(
            collective_id=0, has_side_effects=True, vmem_limit_bytes=58 << 20
        ),
    )(
        queries,
        key_states,
        value_states,
        projector.reshape(4, seg // 4, enc),
        teacher,
        enc_gain,
        enc_bias,
        valid_len,
    )


def solution(mesh):
    rows = P(("grp", "dp"), "seq", None)
    return jax.shard_map(
        shards,
        mesh=mesh,
        in_specs=(rows, rows, rows, P("seq", None), rows, P(), P(), P()),
        out_specs=(rows, rows, rows),
        check_vma=False,
    )
```

```python
import functools

import jax
import jax.numpy as jnp
from jax import lax
from jax.experimental import pallas as pl
from jax.experimental.pallas import tpu as pltpu
from jax.sharding import PartitionSpec as P

HD = 128
SEG = 64
TOK = 2 * SEG
EPS = 1e-06
COEF = 2048.0
LOG2E = 1.4426950408889634
MESH = pl.DeviceIdType.MESH
BF = jnp.bfloat16
F32 = jnp.float32
NT = (((1,), (1,)), ((), ()))


def al(value, step):
    return pl.multiple_of(value, step)


def kernel(
    nz, nr, ndp, bq,
    q_ref, k_ref, v_ref, w_ref, t_ref, gain_ref, bias_ref, len_ref,
    oq_ref, ok_ref, ov_ref,
    stage, t_stage, kb_ref, qh, kh, va, wf, tea, att_h, rows, gsend, gh, gq_h, gk_h, gv_h,
    expo, att_f, linv, aligned, gal, acc_k, acc_v,
    st_send, st_recv, in_send, in_recv, w_send, w_recv, t_send, t_recv, mid_send, mid_recv, out_send, out_recv,
):
    ns = 2 * nz
    total = ns * SEG
    enc = t_ref.shape[-1]
    nx = ndp // 2
    ny = nr // nx
    cw = enc // ny
    nb = total // bq
    per = bq // TOK
    tq = min(4, nr // 2)
    tc = nr // (2 * tq)
    scale = HD ** (-0.5)

    me = lax.axis_index("seq")
    ring = lax.axis_index("grp") * ndp + lax.axis_index("dp")
    z = me // 2
    c = lax.rem(me, 2)

    def on_ring(s):
        return {"seq": s}

    def in_plane(r):
        return {"grp": r // ndp, "dp": lax.rem(r, ndp)}

    def at(r, s):
        return {"grp": r // ndp, "dp": lax.rem(r, ndp), "seq": s}

    barrier = pltpu.get_barrier_semaphore()

    def greet(device):
        pl.semaphore_signal(barrier, 1, device_id=device, device_id_type=MESH)

    @pl.loop(1, ns)
    def _(step):
        greet(on_ring(lax.rem(me + step, ns)))

    @pl.loop(1, nr)
    def _(step):
        greet(in_plane(lax.rem(ring + step, nr)))

    @pl.loop(0, nr)
    def _(step):
        head = lax.rem(ring + step, nr)
        for core in range(2):
            @pl.when((head != ring) & (2 * ring + core != me))
            def _():
                greet(at(head, 2 * ring + core))

    @pl.when(ring == z)
    def _():
        pl.semaphore_wait(barrier, ns - 1 + nr - 1)

    @pl.when(ring != z)
    def _():
        pl.semaphore_wait(barrier, 2 * (ns - 1) + nr - 1)

    def remote(src, dst, ssem, rsem, device):
        return pltpu.make_async_remote_copy(
            src_ref=src, dst_ref=dst, send_sem=ssem, recv_sem=rsem, device_id=device, device_id_type=MESH
        )

    def waiting(view, sem):
        pltpu.make_async_copy(view, view, sem).wait()

    x = lax.axis_index("dp") // 2
    y = lax.axis_index("grp") * 2 + lax.rem(lax.axis_index("dp"), 2)
    band = x
    wcols = pl.ds(al(y * cw, 128), cw)
    own_w = w_ref.at[band, :, wcols]

    @pl.loop(1, nz)
    def _(step):
        there = lax.rem(z + step, nz)
        remote(
            own_w, wf.at[z, c, band, :, wcols], w_send.at[0], w_recv.at[0], on_ring(2 * there + c)
        ).start()

    pltpu.make_async_copy(own_w, wf.at[z, c, band, :, wcols], w_recv.at[0]).start()

    mine = pl.ds(al(me * SEG, SEG), SEG)
    sources = (k_ref, q_ref, v_ref)
    places = (kh.at[mine], qh.at[mine], va.at[mine, pl.ds(0, HD)])

    def scatter_inputs(image):
        for a in range(3):
            @pl.loop(1, nr)
            def _(step):
                head = lax.rem(ring + step, nr)
                remote(
                    sources[a].at[image, :, pl.ds(al(head * HD, HD), HD)], stage.at[image, a, ring],
                    st_send.at[image, a], st_recv.at[image, a], in_plane(head),
                ).start()

            pltpu.make_async_copy(
                sources[a].at[image, :, pl.ds(al(ring * HD, HD), HD)], stage.at[image, a, ring],
                st_recv.at[image, a],
            ).start()

    def pass_inputs(image):
        for a in range(3):
            waiting(stage.at[image, a], st_recv.at[image, a])

            @pl.loop(1, nz)
            def _(step):
                plane = lax.rem(z + step, nz)
                remote(
                    stage.at[image, a, plane], places[a], in_send.at[a], in_recv.at[a],
                    on_ring(2 * plane + image),
                ).start()

            @pl.when(c == image)
            def _():
                pltpu.make_async_copy(stage.at[image, a, z], places[a], in_recv.at[a]).start()

            @pl.when(c != image)
            def _():
                remote(
                    stage.at[image, a, z], places[a], in_send.at[a], in_recv.at[a], on_ring(2 * z + image)
                ).start()

    t_rows = SEG // tq
    t_cols = enc // tc

    def part_of(p):
        rest = lax.rem(p, tq * tc)
        return (
            p // (tq * tc),
            pl.ds(al(rest // tc * t_rows, t_rows), t_rows),
            pl.ds(al(lax.rem(rest, tc) * t_cols, 128), t_cols),
        )

    def scatter_teacher():
        @pl.loop(1, nr)
        def _(step):
            by = lax.rem(ring + step, nr)
            image, rows_at, cols_at = part_of(by)
            remote(
                t_ref.at[image, rows_at, cols_at], t_stage.at[ring], t_send.at[0], t_recv.at[0], in_plane(by)
            ).start()

        image, rows_at, cols_at = part_of(ring)
        pltpu.make_async_copy(t_ref.at[image, rows_at, cols_at], t_stage.at[ring], t_recv.at[0]).start()

    t_image, t_rows_at, t_cols_at = part_of(ring)

    def pass_teacher():
        waiting(t_stage, t_recv.at[0])

        @pl.loop(0, nr)
        def _(step):
            origin = lax.rem(z + nr // 2 + step, nr)
            plane = lax.rem(origin + nr // 2, nr)
            src = t_stage.at[origin]
            dst = tea.at[c, t_rows_at, t_cols_at]
            here = (ring == z) & (plane == z) & (t_image == c)

            @pl.when(here)
            def _():
                pltpu.make_async_copy(src, dst, t_recv.at[1]).start()

            @pl.when(jnp.logical_not(here))
            def _():
                remote(src, dst, t_send.at[1], t_recv.at[1], at(z, 2 * plane + t_image)).start()

    scatter_inputs(0)
    scatter_teacher()
    scatter_inputs(1)
    pass_inputs(0)

    @pl.when(t_image == 0)
    def _():
        pass_teacher()

    waiting(wf.at[:, c, band, :, wcols], w_recv.at[0])
    front, rear = pl.ds(0, nz // 2), pl.ds(nz // 2, nz // 2)

    def along_x(src, sem):
        for step in range(1, nx):
            there = {"dp": lax.rem(x + step, nx) * 2 + lax.rem(y, 2)}
            remote(src, src, w_send.at[sem], w_recv.at[sem], there).start()

    def along_y(src, sem):
        for step in range(1, ny):
            there = lax.rem(y + step, ny)
            remote(
                src, src, w_send.at[sem], w_recv.at[sem], {"grp": there // 2, "dp": x * 2 + lax.rem(there, 2)}
            ).start()

    most_y = pl.ds(0, (ny - 1) * cw)
    most_x = pl.ds(0, max(nx - 1, 1))
    along_x(wf.at[front, c, band, :, wcols], 1)
    along_y(wf.at[rear, c, band, :, wcols], 3)

    pass_inputs(1)

    @pl.when(t_image == 1)
    def _():
        pass_teacher()

    if nx > 1:
        waiting(wf.at[front, c, most_x, :, wcols], w_recv.at[1])
    along_y(wf.at[front, c, :, :, wcols], 4)
    waiting(wf.at[rear, c, band, :, most_y], w_recv.at[3])
    along_x(wf.at[rear, c, band], 5)

    length = len_ref[2 * z + c]
    keys_at = lax.broadcasted_iota(jnp.int32, (1, total), 1)
    kb_ref[...] = jnp.where(keys_at < length, 0.0, -1e30).astype(F32)
    va[:, HD:] = jnp.ones((total, HD), BF)
    acc_k[...] = jnp.zeros_like(acc_k)
    acc_v[...] = jnp.zeros_like(acc_v)

    def swap_w():
        waiting(wf.at[front, c, :, :, most_y], w_recv.at[4])
        if nx > 1:
            waiting(wf.at[rear, c, most_x], w_recv.at[5])
        half = wf.at[:, c]
        remote(half, half, w_send.at[2], w_recv.at[2], on_ring(2 * z + 1 - c)).start()

    @pl.when(c == 1)
    def _():
        swap_w()

    waiting(kh, in_recv.at[0])
    waiting(qh, in_recv.at[1])
    waiting(va.at[:, pl.ds(0, HD)], in_recv.at[2])

    first = ring // per

    @pl.loop(0, nb)
    def _(step):
        block = lax.rem(first + step, nb)
        span = pl.ds(al(block * bq, bq), bq)
        scores = lax.dot_general(qh[span], kh[...], NT, preferred_element_type=F32)
        scores = scores * (scale * LOG2E) + kb_ref[...]
        top = jnp.max(scores, axis=-1, keepdims=True)
        raised = jnp.exp2(scores - top).astype(BF)
        expo[span] = raised
        both = jnp.dot(raised, va[...], preferred_element_type=F32)
        inverse = 1.0 / both[:, HD:]
        attended = both[:, :HD] * inverse
        linv[span] = inverse
        att_f[span] = attended
        att_h[span] = attended.astype(BF)
        for part in range(per):
            there = block * per + part
            src = att_h.at[pl.ds(al(there * TOK, TOK), TOK)]
            dst = rows.at[:, pl.ds(al(ring * HD, HD), HD)]

            @pl.when(there == ring)
            def _():
                pltpu.make_async_copy(src, dst, mid_recv.at[0]).start()

            @pl.when(there != ring)
            def _():
                remote(src, dst, mid_send.at[0], mid_recv.at[0], in_plane(there)).start()

    @pl.when(c == 0)
    def _():
        swap_w()

    waiting(tea, t_recv.at[1])
    for seg in range(2):
        data = tea[seg].astype(F32)
        center = data - jnp.mean(data, axis=-1, keepdims=True)
        spread = jnp.mean(center * center, axis=-1, keepdims=True)
        tea[seg] = (center * lax.rsqrt(spread + EPS) * gain_ref[...][None, :] + bias_ref[...][None, :]).astype(BF)

    waiting(rows, mid_recv.at[0])
    waiting(wf.at[:, 1 - c], w_recv.at[2])

    pieces = enc // 384
    inner = jnp.zeros((TOK, 1), F32)
    own = jnp.zeros((TOK, 1), F32)
    other = jnp.zeros((TOK, 1), F32)
    for piece in range(pieces):
        cols = slice(piece * 384, (piece + 1) * 384)
        weights = wf[:, :, :, :, cols].reshape(nz * HD, 384)
        out = jnp.dot(rows[...], weights, preferred_element_type=F32)
        aligned[:, cols] = out
        tgt = tea[:, :, cols].reshape(TOK, 384).astype(F32)
        inner += jnp.sum(out * tgt, axis=-1, keepdims=True)
        own += jnp.sum(out * out, axis=-1, keepdims=True)
        other += jnp.sum(tgt * tgt, axis=-1, keepdims=True)
    inner = inner / enc
    own = own / enc + EPS
    other = other / enc + EPS
    inverse = lax.rsqrt(own * other)
    cosine = inner * inverse
    token = ring * TOK + lax.broadcasted_iota(jnp.int32, (TOK, 1), 0)
    kept = jnp.where(token < length, -COEF / enc, 0.0).astype(F32)
    left = kept * inverse
    right = kept * (cosine / own)
    for piece in range(pieces):
        cols = slice(piece * 384, (piece + 1) * 384)
        tgt = tea[:, :, cols].reshape(TOK, 384).astype(F32)
        gal[:, cols] = (tgt * left - right * aligned[:, cols]).astype(BF)

    @pl.loop(0, nz // 2)
    def _(step):
        pair = lax.rem(ring // 2 + step, nz // 2)
        weights = wf[pl.ds(pair * 2, 2)].reshape(2 * HD, enc)
        back = lax.dot_general(gal[...], weights, NT, preferred_element_type=F32).astype(BF)
        for part in range(2):
            there = pair * 2 + part
            gsend[there] = back[:, part * HD:(part + 1) * HD]
            src = gsend.at[there]
            dst = gh.at[pl.ds(al(ring * TOK, TOK), TOK)]

            @pl.when(there == ring)
            def _():
                pltpu.make_async_copy(src, dst, mid_recv.at[1]).start()

            @pl.when(there != ring)
            def _():
                remote(src, dst, mid_send.at[1], mid_recv.at[1], in_plane(there)).start()

    waiting(gh, mid_recv.at[1])

    my_cols = pl.ds(al(ring * HD, HD), HD)

    def send_out(src_ref, out_ref, a, s):
        src = src_ref.at[pl.ds(al(s * SEG, SEG), SEG)]
        dst = out_ref.at[c, :, my_cols]

        here = (s == me) & (ring == z)

        @pl.when(here)
        def _():
            pltpu.make_async_copy(src, dst, out_recv.at[a]).start()

        @pl.when(jnp.logical_not(here))
        def _():
            remote(src, dst, out_send.at[a], out_recv.at[a], at(z, s)).start()

    segs = bq // SEG

    @pl.loop(0, nb)
    def _(step):
        block = lax.rem(first + step, nb)
        span = pl.ds(al(block * bq, bq), bq)
        grad = gh[span].astype(F32) * linv[span]
        grad_b = grad.astype(BF)
        delta = jnp.sum(grad_b.astype(F32) * att_f[span], axis=-1, keepdims=True)
        raised = expo[span]
        grad_p = lax.dot_general(grad_b, va[:, :HD], NT, preferred_element_type=F32)
        grad_s = (raised.astype(F32) * (grad_p - delta)).astype(BF)
        acc_v[...] += jnp.dot(grad.T.astype(BF), raised, preferred_element_type=F32)
        acc_k[...] += jnp.dot(qh[span].astype(F32).T.astype(BF), grad_s, preferred_element_type=F32)
        grad_q = jnp.dot(grad_s, kh[...], preferred_element_type=F32)
        gq_h[span] = (grad_q * scale).astype(BF)
        for part in range(segs):
            send_out(gq_h, oq_ref, 0, block * segs + part)

    gv_h[...] = acc_v[...].T.astype(BF)

    @pl.loop(0, ns)
    def _(step):
        send_out(gv_h, ov_ref, 2, lax.rem(me + step, ns))

    gk_h[...] = (acc_k[...] * scale).T.astype(BF)

    @pl.loop(0, ns)
    def _(step):
        send_out(gk_h, ok_ref, 1, lax.rem(me + step, ns))

    waiting(wf.at[pl.ds(0, nz - 1), c, band, :, wcols], w_send.at[0])
    if nx > 1:
        waiting(wf.at[front, c, most_x, :, wcols], w_send.at[1])
        waiting(wf.at[rear, c, most_x], w_send.at[5])
    waiting(wf.at[rear, c, band, :, most_y], w_send.at[3])
    waiting(wf.at[front, c, :, :, most_y], w_send.at[4])
    waiting(wf.at[:, c], w_send.at[2])
    others = pl.ds(0, nr - 1)
    waiting(t_stage.at[others], t_send.at[0])
    t_here = (ring == z) & (t_image == c)

    @pl.when(t_here)
    def _():
        waiting(t_stage.at[others], t_send.at[1])

    @pl.when(jnp.logical_not(t_here))
    def _():
        waiting(t_stage, t_send.at[1])

    for image in range(2):
        for a in range(3):
            waiting(stage.at[image, a, others], st_send.at[image, a])
    most = pl.ds(0, total - SEG)
    for a, buf in enumerate((kh.at[most], qh.at[most], va.at[most, pl.ds(0, HD)])):
        waiting(buf, in_send.at[a])
    waiting(att_h.at[pl.ds(0, total - TOK)], mid_send.at[0])
    waiting(gsend.at[others], mid_send.at[1])
    for a, buf in enumerate((gq_h, gk_h, gv_h)):
        @pl.when(ring == z)
        def _():
            waiting(buf.at[most], out_send.at[a])

        @pl.when(ring != z)
        def _():
            waiting(buf, out_send.at[a])

    for a, buf in enumerate((oq_ref, ok_ref, ov_ref)):
        waiting(buf, out_recv.at[a])


def shards(queries, key_states, value_states, projector, teacher, enc_gain, enc_bias, valid_len):
    ns = lax.axis_size("seq")
    nz = ns // 2
    ndp = lax.axis_size("dp")
    nr = ndp * lax.axis_size("grp")
    count, seg, width = queries.shape
    enc = teacher.shape[-1]
    total = ns * seg
    bq = min(256, total // 2)
    tq = min(4, nr // 2)
    tc = nr // (2 * tq)
    vm = pl.BlockSpec(memory_space=pltpu.VMEM)
    hbm = pl.BlockSpec(memory_space=pl.ANY)
    dma = pltpu.SemaphoreType.DMA
    head = pltpu.VMEM((total, HD), BF)
    head_f = pltpu.VMEM((total, HD), F32)
    out = jax.ShapeDtypeStruct(queries.shape, BF)
    return pl.pallas_call(
        functools.partial(kernel, nz, nr, ndp, bq),
        out_shape=[out, out, out],
        in_specs=[hbm, hbm, hbm, hbm, hbm, vm, vm, pl.BlockSpec(memory_space=pltpu.SMEM)],
        out_specs=[hbm, hbm, hbm],
        scratch_shapes=[
            pltpu.VMEM((2, 3, nr, seg, HD), BF),
            pltpu.VMEM((nr, seg // tq, enc // tc), BF),
            pltpu.VMEM((1, total), F32),
            head,
            head,
            pltpu.VMEM((total, 2 * HD), BF),
            pltpu.VMEM((nz, 2, ndp // 2, 2 * seg // ndp, enc), BF),
            pltpu.VMEM((2, seg, enc), BF),
            head,
            pltpu.VMEM((TOK, width), BF),
            pltpu.VMEM((nz, TOK, HD), BF),
            head,
            head,
            head,
            head,
            pltpu.VMEM((total, total), BF),
            head_f,
            head_f,
            pltpu.VMEM((TOK, enc), F32),
            pltpu.VMEM((TOK, enc), BF),
            pltpu.VMEM((HD, total), F32),
            pltpu.VMEM((HD, total), F32),
            dma((2, 3)),
            dma((2, 3)),
            dma((3,)),
            dma((3,)),
            dma((6,)),
            dma((6,)),
            dma((2,)),
            dma((2,)),
            dma((2,)),
            dma((2,)),
            dma((3,)),
            dma((3,)),
        ],
        compiler_params=pltpu.CompilerParams(
            collective_id=0, has_side_effects=True, vmem_limit_bytes=58 << 20
        ),
    )(
        queries,
        key_states,
        value_states,
        projector.reshape(ndp // 2, 2 * seg // ndp, enc),
        teacher,
        enc_gain,
        enc_bias,
        valid_len,
    )


def solution(mesh):
    rows = P(("grp", "dp"), "seq", None)
    return jax.shard_map(
        shards,
        mesh=mesh,
        in_specs=(rows, rows, rows, P("seq", None), rows, P(), P(), P()),
        out_specs=(rows, rows, rows),
        check_vma=False,
    )
```

```python
import functools

import jax
import jax.numpy as jnp
from jax import lax
from jax.experimental import pallas as pl
from jax.experimental.pallas import tpu as pltpu
from jax.sharding import PartitionSpec as P

HD = 128
SEG = 64
TOK = 2 * SEG
EPS = 1e-06
COEF = 2048.0
LOG2E = 1.4426950408889634
MESH = pl.DeviceIdType.MESH
BF = jnp.bfloat16
F32 = jnp.float32
NT = (((1,), (1,)), ((), ()))


def al(value, step):
    return pl.multiple_of(value, step)


def kernel(
    nz, nr, ndp, bq,
    q_ref, k_ref, v_ref, w_ref, t_ref, gain_ref, bias_ref, len_ref,
    oq_ref, ok_ref, ov_ref,
    stage, t_stage, kb_ref, qh, kh, va, wf, tea, att_h, rows, gsend, gh, gq_h, gk_h, gv_h,
    expo, att_f, linv, aligned, gal, acc_k, acc_v,
    st_send, st_recv, in_send, in_recv, w_send, w_recv, t_send, t_recv, mid_send, mid_recv, out_send, out_recv,
):
    ns = 2 * nz
    total = ns * SEG
    enc = t_ref.shape[-1]
    nx = ndp // 2
    ny = nr // nx
    cw = enc // ny
    nb = total // bq
    per = bq // TOK
    tq = min(4, nr // 2)
    tc = nr // (2 * tq)
    scale = HD ** (-0.5)

    me = lax.axis_index("seq")
    ring = lax.axis_index("grp") * ndp + lax.axis_index("dp")
    z = me // 2
    c = lax.rem(me, 2)

    def on_ring(s):
        return {"seq": s}

    def in_plane(r):
        return {"grp": r // ndp, "dp": lax.rem(r, ndp)}

    def at(r, s):
        return {"grp": r // ndp, "dp": lax.rem(r, ndp), "seq": s}

    barrier = pltpu.get_barrier_semaphore()

    def greet(device):
        pl.semaphore_signal(barrier, 1, device_id=device, device_id_type=MESH)

    @pl.loop(1, ns)
    def _(step):
        greet(on_ring(lax.rem(me + step, ns)))

    @pl.loop(1, nr)
    def _(step):
        greet(in_plane(lax.rem(ring + step, nr)))

    @pl.loop(0, nr)
    def _(step):
        head = lax.rem(ring + step, nr)
        for core in range(2):
            @pl.when((head != ring) & (2 * ring + core != me))
            def _():
                greet(at(head, 2 * ring + core))

    @pl.when(ring == z)
    def _():
        pl.semaphore_wait(barrier, ns - 1 + nr - 1)

    @pl.when(ring != z)
    def _():
        pl.semaphore_wait(barrier, 2 * (ns - 1) + nr - 1)

    def remote(src, dst, ssem, rsem, device):
        return pltpu.make_async_remote_copy(
            src_ref=src, dst_ref=dst, send_sem=ssem, recv_sem=rsem, device_id=device, device_id_type=MESH
        )

    def waiting(view, sem):
        pltpu.make_async_copy(view, view, sem).wait()

    x = lax.axis_index("dp") // 2
    y = lax.axis_index("grp") * 2 + lax.rem(lax.axis_index("dp"), 2)
    band = x
    wcols = pl.ds(al(y * cw, 128), cw)
    own_w = w_ref.at[band, :, wcols]

    @pl.loop(1, nz)
    def _(step):
        there = lax.rem(z + step, nz)
        remote(
            own_w, wf.at[z, c, band, :, wcols], w_send.at[0], w_recv.at[0], on_ring(2 * there + c)
        ).start()

    pltpu.make_async_copy(own_w, wf.at[z, c, band, :, wcols], w_recv.at[0]).start()

    mine = pl.ds(al(me * SEG, SEG), SEG)
    sources = (k_ref, q_ref, v_ref)
    places = (kh.at[mine], qh.at[mine], va.at[mine, pl.ds(0, HD)])

    def scatter_inputs(image):
        for a in range(3):
            @pl.loop(1, nr)
            def _(step):
                head = lax.rem(ring + step, nr)
                remote(
                    sources[a].at[image, :, pl.ds(al(head * HD, HD), HD)], stage.at[image, a, ring],
                    st_send.at[image, a], st_recv.at[image, a], in_plane(head),
                ).start()

            pltpu.make_async_copy(
                sources[a].at[image, :, pl.ds(al(ring * HD, HD), HD)], stage.at[image, a, ring],
                st_recv.at[image, a],
            ).start()

    def pass_inputs(image):
        for a in range(3):
            waiting(stage.at[image, a], st_recv.at[image, a])

            @pl.loop(1, nz)
            def _(step):
                plane = lax.rem(z + step, nz)
                remote(
                    stage.at[image, a, plane], places[a], in_send.at[a], in_recv.at[a],
                    on_ring(2 * plane + image),
                ).start()

            @pl.when(c == image)
            def _():
                pltpu.make_async_copy(stage.at[image, a, z], places[a], in_recv.at[a]).start()

            @pl.when(c != image)
            def _():
                remote(
                    stage.at[image, a, z], places[a], in_send.at[a], in_recv.at[a], on_ring(2 * z + image)
                ).start()

    t_rows = SEG // tq
    t_cols = enc // tc

    def part_of(p):
        rest = lax.rem(p, tq * tc)
        return (
            p // (tq * tc),
            pl.ds(al(rest // tc * t_rows, t_rows), t_rows),
            pl.ds(al(lax.rem(rest, tc) * t_cols, 128), t_cols),
        )

    def scatter_teacher():
        @pl.loop(1, nr)
        def _(step):
            by = lax.rem(ring + step, nr)
            image, rows_at, cols_at = part_of(by)
            remote(
                t_ref.at[image, rows_at, cols_at], t_stage.at[ring], t_send.at[0], t_recv.at[0], in_plane(by)
            ).start()

        image, rows_at, cols_at = part_of(ring)
        pltpu.make_async_copy(t_ref.at[image, rows_at, cols_at], t_stage.at[ring], t_recv.at[0]).start()

    t_image, t_rows_at, t_cols_at = part_of(ring)

    def pass_teacher():
        waiting(t_stage, t_recv.at[0])

        @pl.loop(0, nr)
        def _(step):
            origin = lax.rem(z + nr // 2 + step, nr)
            plane = lax.rem(origin + nr // 2, nr)
            src = t_stage.at[origin]
            dst = tea.at[c, t_rows_at, t_cols_at]
            here = (ring == z) & (plane == z) & (t_image == c)

            @pl.when(here)
            def _():
                pltpu.make_async_copy(src, dst, t_recv.at[1]).start()

            @pl.when(jnp.logical_not(here))
            def _():
                remote(src, dst, t_send.at[1], t_recv.at[1], at(z, 2 * plane + t_image)).start()

    scatter_inputs(0)
    scatter_teacher()
    scatter_inputs(1)
    pass_inputs(0)

    @pl.when(t_image == 0)
    def _():
        pass_teacher()

    waiting(wf.at[:, c, band, :, wcols], w_recv.at[0])
    front, rear = pl.ds(0, nz // 2), pl.ds(nz // 2, nz // 2)

    def along_x(src, sem):
        for step in range(1, nx):
            there = {"dp": lax.rem(x + step, nx) * 2 + lax.rem(y, 2)}
            remote(src, src, w_send.at[sem], w_recv.at[sem], there).start()

    def along_y(src, sem):
        for step in range(1, ny):
            there = lax.rem(y + step, ny)
            remote(
                src, src, w_send.at[sem], w_recv.at[sem], {"grp": there // 2, "dp": x * 2 + lax.rem(there, 2)}
            ).start()

    most_y = pl.ds(0, (ny - 1) * cw)
    most_x = pl.ds(0, max(nx - 1, 1))
    along_x(wf.at[front, c, band, :, wcols], 1)
    along_y(wf.at[rear, c, band, :, wcols], 3)

    pass_inputs(1)

    if nx > 1:
        waiting(wf.at[front, c, most_x, :, wcols], w_recv.at[1])
    along_y(wf.at[front, c, :, :, wcols], 4)
    waiting(wf.at[rear, c, band, :, most_y], w_recv.at[3])
    along_x(wf.at[rear, c, band], 5)

    @pl.when(t_image == 1)
    def _():
        pass_teacher()

    length = len_ref[2 * z + c]
    keys_at = lax.broadcasted_iota(jnp.int32, (1, total), 1)
    kb_ref[...] = jnp.where(keys_at < length, 0.0, -1e30).astype(F32)
    va[:, HD:] = jnp.ones((total, HD), BF)
    acc_k[...] = jnp.zeros_like(acc_k)
    acc_v[...] = jnp.zeros_like(acc_v)

    def swap_w():
        waiting(wf.at[front, c, :, :, most_y], w_recv.at[4])
        if nx > 1:
            waiting(wf.at[rear, c, most_x], w_recv.at[5])
        half = wf.at[:, c]
        remote(half, half, w_send.at[2], w_recv.at[2], on_ring(2 * z + 1 - c)).start()

    @pl.when(c == 1)
    def _():
        swap_w()

    waiting(kh, in_recv.at[0])
    waiting(qh, in_recv.at[1])
    waiting(va.at[:, pl.ds(0, HD)], in_recv.at[2])

    first = ring // per

    @pl.loop(0, nb)
    def _(step):
        block = lax.rem(first + step, nb)
        span = pl.ds(al(block * bq, bq), bq)
        scores = lax.dot_general(qh[span], kh[...], NT, preferred_element_type=F32)
        scores = scores * (scale * LOG2E) + kb_ref[...]
        top = jnp.max(scores, axis=-1, keepdims=True)
        raised = jnp.exp2(scores - top).astype(BF)
        expo[span] = raised
        both = jnp.dot(raised, va[...], preferred_element_type=F32)
        inverse = 1.0 / both[:, HD:]
        attended = both[:, :HD] * inverse
        linv[span] = inverse
        att_f[span] = attended
        att_h[span] = attended.astype(BF)
        for part in range(per):
            there = block * per + part
            src = att_h.at[pl.ds(al(there * TOK, TOK), TOK)]
            dst = rows.at[:, pl.ds(al(ring * HD, HD), HD)]

            @pl.when(there == ring)
            def _():
                pltpu.make_async_copy(src, dst, mid_recv.at[0]).start()

            @pl.when(there != ring)
            def _():
                remote(src, dst, mid_send.at[0], mid_recv.at[0], in_plane(there)).start()

    @pl.when(c == 0)
    def _():
        swap_w()

    waiting(tea, t_recv.at[1])
    for seg in range(2):
        data = tea[seg].astype(F32)
        center = data - jnp.mean(data, axis=-1, keepdims=True)
        spread = jnp.mean(center * center, axis=-1, keepdims=True)
        tea[seg] = (center * lax.rsqrt(spread + EPS) * gain_ref[...][None, :] + bias_ref[...][None, :]).astype(BF)

    waiting(rows, mid_recv.at[0])
    waiting(wf.at[:, 1 - c], w_recv.at[2])

    pieces = enc // 384
    inner = jnp.zeros((TOK, 1), F32)
    own = jnp.zeros((TOK, 1), F32)
    other = jnp.zeros((TOK, 1), F32)
    for piece in range(pieces):
        cols = slice(piece * 384, (piece + 1) * 384)
        weights = wf[:, :, :, :, cols].reshape(nz * HD, 384)
        out = jnp.dot(rows[...], weights, preferred_element_type=F32)
        aligned[:, cols] = out
        tgt = tea[:, :, cols].reshape(TOK, 384).astype(F32)
        inner += jnp.sum(out * tgt, axis=-1, keepdims=True)
        own += jnp.sum(out * out, axis=-1, keepdims=True)
        other += jnp.sum(tgt * tgt, axis=-1, keepdims=True)
    inner = inner / enc
    own = own / enc + EPS
    other = other / enc + EPS
    inverse = lax.rsqrt(own * other)
    cosine = inner * inverse
    token = ring * TOK + lax.broadcasted_iota(jnp.int32, (TOK, 1), 0)
    kept = jnp.where(token < length, -COEF / enc, 0.0).astype(F32)
    left = kept * inverse
    right = kept * (cosine / own)
    for piece in range(pieces):
        cols = slice(piece * 384, (piece + 1) * 384)
        tgt = tea[:, :, cols].reshape(TOK, 384).astype(F32)
        gal[:, cols] = (tgt * left - right * aligned[:, cols]).astype(BF)

    @pl.loop(0, nz // 2)
    def _(step):
        pair = lax.rem(ring // 2 + step, nz // 2)
        weights = wf[pl.ds(pair * 2, 2)].reshape(2 * HD, enc)
        back = lax.dot_general(gal[...], weights, NT, preferred_element_type=F32).astype(BF)
        for part in range(2):
            there = pair * 2 + part
            gsend[there] = back[:, part * HD:(part + 1) * HD]
            src = gsend.at[there]
            dst = gh.at[pl.ds(al(ring * TOK, TOK), TOK)]

            @pl.when(there == ring)
            def _():
                pltpu.make_async_copy(src, dst, mid_recv.at[1]).start()

            @pl.when(there != ring)
            def _():
                remote(src, dst, mid_send.at[1], mid_recv.at[1], in_plane(there)).start()

    waiting(gh, mid_recv.at[1])

    my_cols = pl.ds(al(ring * HD, HD), HD)

    def send_out(src_ref, out_ref, a, s):
        src = src_ref.at[pl.ds(al(s * SEG, SEG), SEG)]
        dst = out_ref.at[c, :, my_cols]

        here = (s == me) & (ring == z)

        @pl.when(here)
        def _():
            pltpu.make_async_copy(src, dst, out_recv.at[a]).start()

        @pl.when(jnp.logical_not(here))
        def _():
            remote(src, dst, out_send.at[a], out_recv.at[a], at(z, s)).start()

    segs = bq // SEG

    @pl.loop(0, nb)
    def _(step):
        block = lax.rem(first + step, nb)
        span = pl.ds(al(block * bq, bq), bq)
        grad = gh[span].astype(F32) * linv[span]
        grad_b = grad.astype(BF)
        delta = jnp.sum(grad_b.astype(F32) * att_f[span], axis=-1, keepdims=True)
        raised = expo[span]
        grad_p = lax.dot_general(grad_b, va[:, :HD], NT, preferred_element_type=F32)
        grad_s = (raised.astype(F32) * (grad_p - delta)).astype(BF)
        acc_v[...] += jnp.dot(grad.T.astype(BF), raised, preferred_element_type=F32)
        acc_k[...] += jnp.dot(qh[span].astype(F32).T.astype(BF), grad_s, preferred_element_type=F32)
        grad_q = jnp.dot(grad_s, kh[...], preferred_element_type=F32)
        gq_h[span] = (grad_q * scale).astype(BF)
        for part in range(segs):
            send_out(gq_h, oq_ref, 0, block * segs + part)

    gv_h[...] = acc_v[...].T.astype(BF)

    @pl.loop(0, ns)
    def _(step):
        send_out(gv_h, ov_ref, 2, lax.rem(me + step, ns))

    gk_h[...] = (acc_k[...] * scale).T.astype(BF)

    @pl.loop(0, ns)
    def _(step):
        send_out(gk_h, ok_ref, 1, lax.rem(me + step, ns))

    waiting(wf.at[pl.ds(0, nz - 1), c, band, :, wcols], w_send.at[0])
    if nx > 1:
        waiting(wf.at[front, c, most_x, :, wcols], w_send.at[1])
        waiting(wf.at[rear, c, most_x], w_send.at[5])
    waiting(wf.at[rear, c, band, :, most_y], w_send.at[3])
    waiting(wf.at[front, c, :, :, most_y], w_send.at[4])
    waiting(wf.at[:, c], w_send.at[2])
    others = pl.ds(0, nr - 1)
    waiting(t_stage.at[others], t_send.at[0])
    t_here = (ring == z) & (t_image == c)

    @pl.when(t_here)
    def _():
        waiting(t_stage.at[others], t_send.at[1])

    @pl.when(jnp.logical_not(t_here))
    def _():
        waiting(t_stage, t_send.at[1])

    for image in range(2):
        for a in range(3):
            waiting(stage.at[image, a, others], st_send.at[image, a])
    most = pl.ds(0, total - SEG)
    for a, buf in enumerate((kh.at[most], qh.at[most], va.at[most, pl.ds(0, HD)])):
        waiting(buf, in_send.at[a])
    waiting(att_h.at[pl.ds(0, total - TOK)], mid_send.at[0])
    waiting(gsend.at[others], mid_send.at[1])
    for a, buf in enumerate((gq_h, gk_h, gv_h)):
        @pl.when(ring == z)
        def _():
            waiting(buf.at[most], out_send.at[a])

        @pl.when(ring != z)
        def _():
            waiting(buf, out_send.at[a])

    for a, buf in enumerate((oq_ref, ok_ref, ov_ref)):
        waiting(buf, out_recv.at[a])


def shards(queries, key_states, value_states, projector, teacher, enc_gain, enc_bias, valid_len):
    ns = lax.axis_size("seq")
    nz = ns // 2
    ndp = lax.axis_size("dp")
    nr = ndp * lax.axis_size("grp")
    count, seg, width = queries.shape
    enc = teacher.shape[-1]
    total = ns * seg
    bq = min(256, total // 2)
    tq = min(4, nr // 2)
    tc = nr // (2 * tq)
    vm = pl.BlockSpec(memory_space=pltpu.VMEM)
    hbm = pl.BlockSpec(memory_space=pl.ANY)
    dma = pltpu.SemaphoreType.DMA
    head = pltpu.VMEM((total, HD), BF)
    head_f = pltpu.VMEM((total, HD), F32)
    out = jax.ShapeDtypeStruct(queries.shape, BF)
    return pl.pallas_call(
        functools.partial(kernel, nz, nr, ndp, bq),
        out_shape=[out, out, out],
        in_specs=[hbm, hbm, hbm, hbm, hbm, vm, vm, pl.BlockSpec(memory_space=pltpu.SMEM)],
        out_specs=[hbm, hbm, hbm],
        scratch_shapes=[
            pltpu.VMEM((2, 3, nr, seg, HD), BF),
            pltpu.VMEM((nr, seg // tq, enc // tc), BF),
            pltpu.VMEM((1, total), F32),
            head,
            head,
            pltpu.VMEM((total, 2 * HD), BF),
            pltpu.VMEM((nz, 2, ndp // 2, 2 * seg // ndp, enc), BF),
            pltpu.VMEM((2, seg, enc), BF),
            head,
            pltpu.VMEM((TOK, width), BF),
            pltpu.VMEM((nz, TOK, HD), BF),
            head,
            head,
            head,
            head,
            pltpu.VMEM((total, total), BF),
            head_f,
            head_f,
            pltpu.VMEM((TOK, enc), F32),
            pltpu.VMEM((TOK, enc), BF),
            pltpu.VMEM((HD, total), F32),
            pltpu.VMEM((HD, total), F32),
            dma((2, 3)),
            dma((2, 3)),
            dma((3,)),
            dma((3,)),
            dma((6,)),
            dma((6,)),
            dma((2,)),
            dma((2,)),
            dma((2,)),
            dma((2,)),
            dma((3,)),
            dma((3,)),
        ],
        compiler_params=pltpu.CompilerParams(
            collective_id=0, has_side_effects=True, vmem_limit_bytes=58 << 20
        ),
    )(
        queries,
        key_states,
        value_states,
        projector.reshape(ndp // 2, 2 * seg // ndp, enc),
        teacher,
        enc_gain,
        enc_bias,
        valid_len,
    )


def solution(mesh):
    rows = P(("grp", "dp"), "seq", None)
    return jax.shard_map(
        shards,
        mesh=mesh,
        in_specs=(rows, rows, rows, P("seq", None), rows, P(), P(), P()),
        out_specs=(rows, rows, rows),
        check_vma=False,
    )
```
